512 devices in a mesh: chan: 16 (over z), tm: 32 (over y, x, core).
Axes of the slice: x: 4, y: 4, z: 16, core: 2. Of those that a mesh axis runs over, the one named last changes fastest.
Arguments:
- traces: bfloat16 [64, 1920, 2048], P('tm', None, 'chan'), may hold values from -6 to 6
- band_bins: int32 [512], replicated, may hold values from 1 to 959, as said below
- partners: int32 [16, 4], P('chan'), may hold values from 0 to 15, as said below
- partner_counts: int32 [16], P('chan'), may hold values from 1 to 4, as said below
Outputs:
- cross_spectra: bfloat16 [16, 4, 512, 2, 128, 128], P('chan', None, 'tm')
The draws below stay inside these ranges and needn't reach their ends.
Inputs may be any that keep to these rules, and one draw needn't show every extreme that they name: `band_bins`: 512 distinct bin numbers in no particular order. `partners`: row b lists b itself first, then the other blocks whose pair with b is listed at b, each of them b + 1, b - 1 or b + 2. A pair of blocks one apart is listed at one of the two, a pair two apart at the lower one, so every pair of blocks at most two apart is listed exactly once. Slots from partner_counts[b] on hold b. `partner_counts`: the number of listed partners of block b, b itself included.
All inputs are finite; a program needn't handle non-finite values.
Results may differ from the reference program's by a relative error of at most 0.0063.
Values may be sent and summed in bfloat16 or wider, within the bound.
A program may use at most 64 MiB of HBM per device.

```python
import math
import jax
import jax.numpy as jnp
from jax import lax

SAMPLES = 1920
NF = 512
CH = 128
MAXP = 4
WINDOWS = 64
BLOCKS = 16
CHANNELS = 2048


def pair_lists(key):
    flips = jax.random.randint(key, (BLOCKS,), 0, 2).astype(jnp.int32)
    flips = flips.at[0].set(0).at[1].set(1)
    number = jnp.arange(BLOCKS, dtype=jnp.int32)
    earlier = jnp.concatenate([jnp.ones((1,), jnp.int32), flips[:-1]])
    forward_one = flips * (number + 1 < BLOCKS).astype(jnp.int32)
    backward_one = (1 - earlier) * (number >= 1).astype(jnp.int32)
    forward_two = (number + 2 < BLOCKS).astype(jnp.int32)
    valid = jnp.stack([jnp.ones_like(number), forward_one, backward_one, forward_two], axis=1)
    candidates = jnp.stack([number, number + 1, number - 1, number + 2], axis=1)
    position = jnp.cumsum(valid, axis=1) - 1
    slot_index = jnp.arange(MAXP, dtype=jnp.int32)
    hit = ((valid[:, :, None] == 1) & (position[:, :, None] == slot_index[None, None, :])).astype(jnp.int32)
    filled = jnp.sum(hit, axis=1)
    chosen = jnp.sum(candidates[:, :, None] * hit, axis=1) + number[:, None] * (1 - filled)
    return (chosen.astype(jnp.int32), jnp.sum(valid, axis=1).astype(jnp.int32))


def draw_partners(key, part):
    return pair_lists(key)[0]


def draw_partner_counts(key, part):
    return pair_lists(key)[1]


def draw_band_bins(key, part):
    key = jax.random.fold_in(key, 11)
    inner = jax.random.permutation(key, SAMPLES // 2 - 3).astype(jnp.int32) + 2
    chosen = inner[:NF - 2]
    ends = jnp.array([1, SAMPLES // 2 - 1], jnp.int32)
    return jnp.concatenate([ends, chosen])


def steps_of(rng, extent, shards, smallest, largest):
    def one(dim, shards_of):
        heights = jax.random.uniform(jax.random.fold_in(jax.random.fold_in(rng, 6), dim), (shards_of,), jnp.float32, smallest / len(shards), largest / len(shards))
        return jnp.repeat(jnp.exp(heights), extent[dim] // shards_of).reshape((-1,) + (1,) * (len(extent) - dim - 1))

    loudness = one(*shards[0])
    for cut in shards[1:]:
        loudness = loudness * one(*cut)
    return loudness


def normal_values(key, extent, spread, bound, split=(), held_as=jnp.bfloat16):
    values = jax.random.normal(key, extent, jnp.float32) * spread
    if len(split) > 0:
        values = steps_of(key, extent, split, -0.22, 0.18) * values
    return jnp.clip(values, min=-bound, max=bound).astype(held_as)


def setup_inputs(seed: int = 0) -> dict:
    streams_of = jax.random.split(jax.random.key(seed), 5)
    return {
        "traces": normal_values(streams_of[0], (WINDOWS, SAMPLES, CHANNELS), 1.0, 6.0, ((0, 32), (2, 16))),
        "band_bins": draw_band_bins(jax.random.fold_in(streams_of[4], 71), 0),
        "partners": draw_partners(jax.random.fold_in(streams_of[4], 71), 0),
        "partner_counts": draw_partner_counts(jax.random.fold_in(streams_of[4], 71), 0),
    }


def band_table(band_bins, samples):
    band_count = band_bins.shape[0]
    sample_index = jnp.arange(samples, dtype=jnp.int32)
    phase_index = band_bins[:, None] * sample_index[None, :] % samples
    angles = phase_index.astype(jnp.float32) * (2.0 * math.pi / samples)
    stacked = jnp.stack([jnp.cos(angles), -jnp.sin(angles)], axis=1)
    return stacked.reshape(2 * band_count, samples).astype(jnp.bfloat16)

def reference(traces, band_bins, partners, partner_counts):
    transform_table = band_table(band_bins, SAMPLES)

    def whiten(window):
        spectra = jnp.dot(transform_table, window, preferred_element_type=jnp.float32)
        band_power = lax.optimization_barrier(jnp.mean(spectra * spectra, axis=0))
        return (spectra * lax.rsqrt(band_power + 1e-06)).astype(jnp.bfloat16)
    whitened = lax.map(whiten, traces).reshape(WINDOWS, NF, 2, CHANNELS)

    def block_slice(block_number):
        start = (block_number * CH).astype(jnp.int32)
        return lax.dynamic_slice_in_dim(whitened, start, CH, 3).astype(jnp.float32)

    def one_block(block_number):
        local_block = block_slice(block_number)
        slot_rows = []
        for slot_index in range(MAXP):
            partner_block = block_slice(partners[block_number, slot_index])
            swapped = jnp.stack([-partner_block[:, :, 1], partner_block[:, :, 0]], axis=2)
            real_part = jnp.einsum('wkpc,wkpd->kcd', local_block, partner_block, precision=lax.Precision.HIGHEST)
            imag_part = jnp.einsum('wkpc,wkpd->kcd', local_block, swapped, precision=lax.Precision.HIGHEST)
            keep_slot = (slot_index < partner_counts[block_number]).astype(jnp.float32)
            both_parts = jnp.stack([real_part, imag_part], axis=1) * keep_slot
            slot_rows.append(both_parts.astype(jnp.bfloat16))
        return jnp.stack(slot_rows)
    return lax.map(one_block, jnp.arange(BLOCKS, dtype=jnp.int32))
```

```python
import functools
import math

import jax
import jax.numpy as jnp
from jax import lax
from jax.experimental import pallas as pl
from jax.experimental.pallas import tpu as pltpu
from jax.sharding import PartitionSpec as P

LANES = 128
MESH = pl.DeviceIdType.MESH


def unit_circle(turns_number, samples):
    quarter = samples // 4
    quadrant = jnp.floor(turns_number * (1.0 / quarter) + 0.5)
    x = (turns_number - quadrant * quarter) * (math.pi / 2 / quarter)
    y = x * x
    sine = x * (1 + y * (-1 / 6 + y * (1 / 120 + y * (-1 / 5040 + y * (1 / 362880)))))
    cosine = 1 + y * (-1 / 2 + y * (1 / 24 + y * (-1 / 720 + y * (1 / 40320 + y * (-1 / 3628800)))))
    which = quadrant.astype(jnp.int32)
    odd = (which & 1) == 1
    c = jnp.where(odd, sine, cosine)
    s = jnp.where(odd, cosine, sine)
    c = jnp.where(((which + 1) & 2) == 2, -c, c)
    s = jnp.where((which & 2) == 2, -s, s)
    return c, s


def spectra_kernel(bins_ref, traces_ref, send_ref, table_ref, spectra_ref):
    windows, samples, channels = traces_ref.shape
    groups, group = bins_ref.shape
    bin_count = groups * group
    lane = lax.broadcasted_iota(jnp.int32, (group, LANES), 1).astype(jnp.float32)
    both = jnp.concatenate([traces_ref[w] for w in range(windows)], axis=1)
    power = jnp.zeros((1, windows * channels), jnp.float32)
    for g in range(groups):
        row = bins_ref[g : g + 1, :].astype(jnp.float32)
        number = jnp.broadcast_to(row, (group, group)).T
        number = number[:, :LANES]
        c, s = unit_circle(number * lane, samples)
        step_c, step_s = unit_circle(number * float(LANES), samples)
        for q in range(samples // LANES):
            table_ref[g % 2, :group, q * LANES : (q + 1) * LANES] = c.astype(jnp.bfloat16)
            table_ref[g % 2, group:, q * LANES : (q + 1) * LANES] = (-s).astype(jnp.bfloat16)
            c, s = c * step_c - s * step_s, s * step_c + c * step_s
        y = jnp.dot(table_ref[g % 2], both, preferred_element_type=jnp.float32)
        spectra_ref[g] = y
        power = power + jnp.sum(y * y, axis=0, keepdims=True)
    scale = lax.rsqrt(power * (1.0 / (2 * bin_count)) + 1e-06)
    per = group // 16
    for g in range(groups):
        y = (spectra_ref[g] * scale).reshape(2, per, 2, 8, windows * channels)
        for h in range(2):
            parts = []
            for w in range(windows):
                for p in range(2):
                    parts.append(y[p, :, h, :, w * channels : (w + 1) * channels])
            send_ref[h, g * per : (g + 1) * per] = jnp.concatenate(parts, axis=1).astype(jnp.bfloat16)


def exchange_kernel(tm_count, send_ref, out_ref, held, wide, regrouped, local_sem, out_sem, in_sem,
                    down_send, down_recv, up_send, up_recv, relay_send, relay_recv):
    me = lax.axis_index("tm")
    block = lax.axis_index("chan")
    blocks = lax.axis_size("chan")
    has_below = block > 0
    has_above = block < blocks - 1
    pieces = down_send.shape[0]
    bins = regrouped.shape[0]
    size = bins // pieces
    rows = send_ref.shape[2]
    channels = send_ref.shape[3]
    windows = rows // 16 * tm_count

    barrier = pltpu.get_barrier_semaphore()

    @pl.loop(1, tm_count)
    def _(r):
        pl.semaphore_signal(barrier, inc=1, device_id=(block, lax.rem(me + r, tm_count)), device_id_type=MESH)

    @pl.when(has_below)
    def _():
        pl.semaphore_signal(barrier, inc=1, device_id=(block - 1, me), device_id_type=MESH)

    @pl.when(has_above)
    def _():
        pl.semaphore_signal(barrier, inc=1, device_id=(block + 1, me), device_id_type=MESH)

    others = has_below.astype(jnp.int32) + has_above.astype(jnp.int32)
    pl.semaphore_wait(barrier, tm_count - 1 + others)

    for h in range(2):
        @pl.loop(1, tm_count)
        def _(r):
            to = lax.rem(me + r, tm_count)
            pltpu.make_async_remote_copy(
                src_ref=send_ref.at[h, to], dst_ref=held.at[h, me],
                send_sem=out_sem.at[h], recv_sem=in_sem.at[h],
                device_id=(block, to), device_id_type=MESH).start()

        held[h, me] = send_ref[h, me]

    def down(q):
        part = pl.ds(q * size, size)
        return pltpu.make_async_remote_copy(
            src_ref=regrouped.at[part], dst_ref=out_ref.at[1, part],
            send_sem=down_send.at[q], recv_sem=down_recv.at[q],
            device_id=(block - 1, me), device_id_type=MESH)

    def up(q):
        part = pl.ds(q * size, size)
        return pltpu.make_async_remote_copy(
            src_ref=regrouped.at[part], dst_ref=out_ref.at[2, part],
            send_sem=up_send.at[q], recv_sem=up_recv.at[q],
            device_id=(block + 1, me), device_id_type=MESH)

    def relay(q):
        part = pl.ds(q * size, size)
        return pltpu.make_async_remote_copy(
            src_ref=out_ref.at[1, part], dst_ref=out_ref.at[3, part],
            send_sem=relay_send.at[q], recv_sem=relay_recv.at[q],
            device_id=(block - 1, me), device_id_type=MESH)

    def keep(q):
        part = pl.ds(q * size, size)
        return pltpu.make_async_copy(regrouped.at[part], out_ref.at[0, part], local_sem.at[q])

    for h in range(2):
        whole = held.at[h, pl.ds(0, tm_count - 1)]
        pltpu.make_async_copy(whole, whole, in_sem.at[h]).wait()
        wide[...] = held[h].astype(jnp.float32).reshape(tm_count * rows, channels)
        for q in range(h * pieces // 2, (h + 1) * pieces // 2):
            for j in range(size):
                at = q * size + j
                for p in range(2):
                    start = at - 8 * h + 8 * p
                    lines = wide[pl.ds(start, windows, stride=16), :]
                    regrouped[at, p * windows : (p + 1) * windows, :] = lines.astype(jnp.bfloat16)

            @pl.when(has_below)
            def _():
                down(q).start()

            @pl.when(has_above)
            def _():
                up(q).start()

            keep(q).start()

    for q in range(pieces):
        @pl.when(has_above)
        def _():
            down(q).wait_recv()

        @pl.when(has_above & has_below)
        def _():
            relay(q).start()

    for q in range(pieces):
        keep(q).wait()

        @pl.when(has_below)
        def _():
            up(q).wait_recv()
            down(q).wait_send()

        @pl.when(has_above)
        def _():
            up(q).wait_send()

        @pl.when(block < blocks - 2)
        def _():
            relay(q).wait_recv()

        @pl.when(has_above & has_below)
        def _():
            relay(q).wait_send()

    for h in range(2):
        whole = held.at[h, pl.ds(0, tm_count - 1)]
        pltpu.make_async_copy(whole, whole, out_sem.at[h]).wait()


def product_kernel(partners_ref, counts_ref, blocks_ref, out_ref):
    block = lax.axis_index("chan")
    bins, depth, channels = blocks_ref.shape[1:]
    half = depth // 2
    slots = out_ref.shape[1]
    where_from = []
    for slot in range(slots):
        offset = partners_ref[0, slot] - block
        where_from.append(jnp.where(offset == 1, 1, jnp.where(offset == -1, 2, jnp.where(offset == 2, 3, 0))))
    for k in range(bins):
        own = blocks_ref[0, k]
        turned = jnp.concatenate([own[half:], -own[:half]], axis=0)
        left = jnp.concatenate([own, turned], axis=1)
        for slot in range(slots):
            @pl.when(slot < counts_ref[0])
            def _():
                other = blocks_ref[where_from[slot], k]
                both = lax.dot_general(left, other, (((0,), (0,)), ((), ())), preferred_element_type=jnp.float32)
                out_ref[0, slot, k] = both.astype(jnp.bfloat16).reshape(2, channels, channels)

            @pl.when(slot >= counts_ref[0])
            def _():
                out_ref[0, slot, k] = jnp.zeros((2, channels, channels), jnp.bfloat16)


def body(traces, band_bins, partners, partner_counts):
    windows, samples, channels = traces.shape
    bin_count = band_bins.shape[0]
    tm_count = lax.axis_size("tm")
    group = min(128, bin_count)
    groups = bin_count // group
    bins = bin_count // tm_count
    rows = 16 * windows
    send = pl.pallas_call(
        spectra_kernel,
        out_shape=jax.ShapeDtypeStruct((2, tm_count, rows, channels), jnp.bfloat16),
        in_specs=[pl.BlockSpec(memory_space=pltpu.VMEM)] * 2,
        out_specs=pl.BlockSpec(memory_space=pltpu.VMEM),
        scratch_shapes=[
            pltpu.VMEM((2, 2 * group, samples), jnp.bfloat16),
            pltpu.VMEM((groups, 2 * group, windows * channels), jnp.float32),
        ],
        compiler_params=pltpu.CompilerParams(vmem_limit_bytes=48 << 20),
        name="spectra",
    )(band_bins.reshape(groups, group), traces)

    pieces = 4
    depth = 2 * windows * tm_count
    blocks = pl.pallas_call(
        functools.partial(exchange_kernel, tm_count),
        out_shape=jax.ShapeDtypeStruct((4, bins, depth, channels), jnp.bfloat16),
        in_specs=[pl.BlockSpec(memory_space=pltpu.VMEM)],
        out_specs=pl.BlockSpec(memory_space=pl.ANY),
        scratch_shapes=[
            pltpu.VMEM((2, tm_count, rows, channels), jnp.bfloat16),
            pltpu.VMEM((tm_count * rows, channels), jnp.float32),
            pltpu.VMEM((bins, depth, channels), jnp.bfloat16),
            pltpu.SemaphoreType.DMA((pieces,)),
            pltpu.SemaphoreType.DMA((2,)),
            pltpu.SemaphoreType.DMA((2,)),
        ] + [pltpu.SemaphoreType.DMA((pieces,))] * 6,
        compiler_params=pltpu.CompilerParams(
            collective_id=0, has_side_effects=True, vmem_limit_bytes=48 << 20),
        name="exchange",
    )(send)

    step = 4
    return pl.pallas_call(
        product_kernel,
        grid=(bins // step,),
        out_shape=jax.ShapeDtypeStruct((1, 4, bins, 2, channels, channels), jnp.bfloat16),
        in_specs=[
            pl.BlockSpec(memory_space=pltpu.SMEM),
            pl.BlockSpec(memory_space=pltpu.SMEM),
            pl.BlockSpec((4, step, depth, channels), lambda i: (0, i, 0, 0)),
        ],
        out_specs=pl.BlockSpec((1, 4, step, 2, channels, channels), lambda i: (0, 0, i, 0, 0, 0)),
        compiler_params=pltpu.CompilerParams(vmem_limit_bytes=48 << 20),
        name="products",
    )(partners, partner_counts, blocks)


def solution(mesh):
    placed = (P("tm", None, "chan"), P(), P("chan", None), P("chan"))
    return jax.shard_map(
        body,
        mesh=mesh,
        in_specs=placed,
        out_specs=P("chan", None, "tm", None, None, None),
        check_vma=False,
    )
```

```python
import functools
import math

import jax
import jax.numpy as jnp
from jax import lax
from jax.experimental import pallas as pl
from jax.experimental.pallas import tpu as pltpu
from jax.sharding import PartitionSpec as P

LANES = 128
MESH = pl.DeviceIdType.MESH


def unit_circle(turns_number, samples):
    quarter = samples // 4
    quadrant = jnp.floor(turns_number * (1.0 / quarter) + 0.5)
    x = (turns_number - quadrant * quarter) * (math.pi / 2 / quarter)
    y = x * x
    sine = x * (1 + y * (-1 / 6 + y * (1 / 120 + y * (-1 / 5040 + y * (1 / 362880)))))
    cosine = 1 + y * (-1 / 2 + y * (1 / 24 + y * (-1 / 720 + y * (1 / 40320 + y * (-1 / 3628800)))))
    which = quadrant.astype(jnp.int32)
    odd = (which & 1) == 1
    c = jnp.where(odd, sine, cosine)
    s = jnp.where(odd, cosine, sine)
    c = jnp.where(((which + 1) & 2) == 2, -c, c)
    s = jnp.where((which & 2) == 2, -s, s)
    return c, s


def exchange_kernel(tm_count, bins_hbm, traces_hbm, made_ref, left_ref, last_ref, bins_ref, traces_ref, table_ref, spectra_ref,
                    send_ref, held, upper, lower, second, wide, block_ref, load_sem, out_sem, in_sem,
                    down_send, down_recv, up_send, up_recv, relay_send, relay_recv):
    me = lax.axis_index("tm")
    block = lax.axis_index("chan")
    blocks = lax.axis_size("chan")
    has_below = block > 0
    has_above = block < blocks - 1
    windows, samples, channels = traces_ref.shape
    groups, group = bins_ref.shape
    bin_count = groups * group
    rows = send_ref.shape[1]
    chips = tm_count // 2
    side = math.isqrt(chips)
    chip = me // 2
    core = lax.rem(me, 2)
    chip_y = chip // side
    chip_x = lax.rem(chip, side)

    barrier = pltpu.get_barrier_semaphore()

    load_bins = pltpu.make_async_copy(bins_hbm, bins_ref, load_sem.at[0])
    load_traces = pltpu.make_async_copy(traces_hbm, traces_ref, load_sem.at[1])
    load_bins.start()
    load_traces.start()

    @pl.loop(1, tm_count)
    def _(r):
        pl.semaphore_signal(barrier, inc=1, device_id=(block, lax.rem(me + r, tm_count)), device_id_type=MESH)

    @pl.when(has_below)
    def _():
        pl.semaphore_signal(barrier, inc=1, device_id=(block - 1, me), device_id_type=MESH)

    @pl.when(has_above)
    def _():
        pl.semaphore_signal(barrier, inc=1, device_id=(block + 1, me), device_id_type=MESH)

    lane = lax.broadcasted_iota(jnp.int32, (group, LANES), 1).astype(jnp.float32)
    load_bins.wait()
    power = jnp.zeros((1, windows * channels), jnp.float32)
    for g in range(groups):
        row = bins_ref[g : g + 1, :].astype(jnp.float32)
        number = jnp.broadcast_to(row, (group, group)).T
        c, s = unit_circle(number * lane, samples)
        step_c, step_s = unit_circle(number * float(LANES), samples)
        for q in range(samples // LANES):
            table_ref[g % 2, :group, q * LANES : (q + 1) * LANES] = c.astype(jnp.bfloat16)
            table_ref[g % 2, group:, q * LANES : (q + 1) * LANES] = (-s).astype(jnp.bfloat16)
            c, s = c * step_c - s * step_s, s * step_c + c * step_s
        if g == 0:
            load_traces.wait()
        both = jnp.concatenate([traces_ref[w] for w in range(windows)], axis=1)
        y = jnp.dot(table_ref[g % 2], both, preferred_element_type=jnp.float32)
        spectra_ref[g] = y
        power = power + jnp.sum(y * y, axis=0, keepdims=True)
    scale = lax.rsqrt(power * (1.0 / (2 * bin_count)) + 1e-06)
    per = group // 16
    for g in range(groups):
        y = (spectra_ref[g] * scale).reshape(2, per, 2, 8, windows * channels)
        parts = []
        for w in range(windows):
            for h in range(2):
                for p in range(2):
                    parts.append(y[p, :, h, :, w * channels : (w + 1) * channels])
        send_ref[g * per : (g + 1) * per] = jnp.concatenate(parts, axis=1).astype(jnp.bfloat16)

    others = has_below.astype(jnp.int32) + has_above.astype(jnp.int32)
    pl.semaphore_wait(barrier, tm_count - 1 + others)

    def fold(d):
        return d + d // 2 - 2 * (d // 3)

    def chip_at(step, sign):
        dy, dx = fold(step // side), fold(lax.rem(step, side))
        return lax.rem(chip_y + sign * dy + side, side) * side + lax.rem(chip_x + sign * dx + side, side)

    def spread(to):
        pltpu.make_async_remote_copy(
            src_ref=send_ref.at[to], dst_ref=held.at[me],
            send_sem=out_sem, recv_sem=in_sem.at[chip],
            device_id=(block, to), device_id_type=MESH).start()

    def pair(ref, f):
        return ref.at[pl.ds(f * 2, 2)]

    def down(f):
        return pltpu.make_async_remote_copy(
            src_ref=pair(held, f), dst_ref=pair(upper, f), send_sem=down_send, recv_sem=down_recv.at[f],
            device_id=(block - 1, me), device_id_type=MESH)

    def up(f):
        return pltpu.make_async_remote_copy(
            src_ref=pair(held, f), dst_ref=pair(lower, f), send_sem=up_send, recv_sem=up_recv,
            device_id=(block + 1, me), device_id_type=MESH)

    def relay(f):
        return pltpu.make_async_remote_copy(
            src_ref=pair(upper, f), dst_ref=pair(second, f), send_sem=relay_send, recv_sem=relay_recv,
            device_id=(block - 1, me), device_id_type=MESH)

    def forward(f):
        @pl.when(has_below)
        def _():
            down(f).start()

        @pl.when(has_above)
        def _():
            up(f).start()

    def wait_for(ref, sem):
        pltpu.make_async_copy(ref, ref, sem).wait()

    spread(chip * 2 + 1 - core)

    @pl.loop(1, chips)
    def _(step):
        to = chip_at(step, 1)
        spread(to * 2 + core)
        spread(to * 2 + 1 - core)

    held[me] = send_ref[me]
    wait_for(held.at[0], in_sem.at[chip])
    forward(chip)

    @pl.loop(1, chips)
    def _(step):
        f = chip_at(step, -1)
        wait_for(pair(held, 0), in_sem.at[f])
        forward(f)

    total = tm_count * windows

    def regroup(ref, to_ref):
        wide[...] = ref[...].astype(jnp.float32).reshape(tm_count * rows, channels)
        for j in range(16):
            for p in range(2):
                lines = wide[pl.ds(j // 8 * 16 + p * 8 + j % 8, total, stride=32), :]
                to_ref[j, p * total : (p + 1) * total, :] = lines.astype(jnp.bfloat16)

    def products(where):
        @pl.loop(0, 16)
        def _(j):
            both = jnp.dot(left_ref[j], block_ref[j], preferred_element_type=jnp.float32)
            made_ref[where, j] = both.astype(jnp.bfloat16).reshape(2, channels, channels)

    @pl.when(has_above)
    def _():
        @pl.loop(0, chips)
        def _(step):
            f = chip_at(step, -1)
            wait_for(pair(upper, 0), down_recv.at[f])

            @pl.when(has_below)
            def _():
                relay(f).start()

    regroup(held, block_ref)

    @pl.loop(0, 16)
    def _(j):
        own = block_ref[j]
        left_ref[j, :channels, :] = own.T
        left_ref[j, channels:, :] = jnp.concatenate([own[total:], -own[:total]], axis=0).T

    products(0)

    @pl.when(has_above)
    def _():
        regroup(upper, block_ref)
        products(1)

    @pl.when(has_below)
    def _():
        wait_for(lower, up_recv)
        regroup(lower, block_ref)
        products(2)

    wait_for(held.at[pl.ds(0, tm_count - 1)], out_sem)

    @pl.when(has_below)
    def _():
        wait_for(held, down_send)

    @pl.when(has_above)
    def _():
        wait_for(held, up_send)

    @pl.when(has_above & has_below)
    def _():
        wait_for(held, relay_send)

    @pl.when(block < blocks - 2)
    def _():
        wait_for(second, relay_recv)
        regroup(second, last_ref)


def place_kernel(counts_ref, partners_hbm, made_ref, left_ref, last_ref, out_hbm,
                 partners_ref, product_ref, zero_ref, load_sem, out_sem):
    block = lax.axis_index("chan")
    bins, _, channels = last_ref.shape
    slots = out_hbm.shape[1]
    load_partners = pltpu.make_async_copy(partners_hbm, partners_ref, load_sem)
    load_partners.start()
    pltpu.make_async_copy(made_ref.at[0], out_hbm.at[0, 0], out_sem).start()
    zero_ref[...] = jnp.zeros_like(zero_ref)
    load_partners.wait()
    for slot in range(1, slots):
        offset = partners_ref[0, slot] - block
        listed = slot < counts_ref[0]

        @pl.when(listed & (offset == 1))
        def _():
            pltpu.make_async_copy(made_ref.at[1], out_hbm.at[0, slot], out_sem).start()

        @pl.when(listed & (offset == -1))
        def _():
            pltpu.make_async_copy(made_ref.at[2], out_hbm.at[0, slot], out_sem).start()

        @pl.when(jnp.logical_not(listed))
        def _():
            for k in range(0, bins, zero_ref.shape[0]):
                to = out_hbm.at[0, slot, pl.ds(k, zero_ref.shape[0])]
                pltpu.make_async_copy(zero_ref, to, out_sem).start()

    for slot in range(1, slots):
        @pl.when((slot < counts_ref[0]) & (partners_ref[0, slot] - block == 2))
        def _():
            for k in range(bins):
                both = jnp.dot(left_ref[k], last_ref[k], preferred_element_type=jnp.float32)
                product_ref[k] = both.astype(jnp.bfloat16).reshape(2, channels, channels)
                if k % 2 == 1:
                    part = pl.ds(k - 1, 2)
                    pltpu.make_async_copy(product_ref.at[part], out_hbm.at[0, slot, part], out_sem).start()

    for slot in range(slots):
        pltpu.make_async_copy(made_ref.at[0], out_hbm.at[0, slot], out_sem).wait()


def body(traces, band_bins, partners, partner_counts):
    windows, samples, channels = traces.shape
    bin_count = band_bins.shape[0]
    tm_count = lax.axis_size("tm")
    group = min(128, bin_count)
    groups = bin_count // group
    bins = bin_count // tm_count
    rows = 32 * windows
    chips = tm_count // 2
    depth = 2 * windows * tm_count
    dma = pltpu.SemaphoreType.DMA
    buffer = pltpu.VMEM((tm_count, rows, channels), jnp.bfloat16)
    made, left, last = pl.pallas_call(
        functools.partial(exchange_kernel, tm_count),
        out_shape=[
            pltpu.VMEM((3, bins, 2, channels, channels), jnp.bfloat16),
            pltpu.VMEM((bins, 2 * channels, depth), jnp.bfloat16),
            pltpu.VMEM((bins, depth, channels), jnp.bfloat16),
        ],
        in_specs=[pl.BlockSpec(memory_space=pltpu.HBM)] * 2,
        out_specs=[pl.BlockSpec(memory_space=pltpu.VMEM)] * 3,
        scratch_shapes=[
            pltpu.VMEM((groups, group), jnp.int32),
            pltpu.VMEM((windows, samples, channels), jnp.bfloat16),
            pltpu.VMEM((2, 2 * group, samples), jnp.bfloat16),
            pltpu.VMEM((groups, 2 * group, windows * channels), jnp.float32),
            buffer, buffer, buffer, buffer, buffer,
            pltpu.VMEM((tm_count * rows, channels), jnp.float32),
            pltpu.VMEM((bins, depth, channels), jnp.bfloat16),
            dma((2,)), dma, dma((chips,)),
            dma, dma((chips,)), dma, dma, dma, dma,
        ],
        compiler_params=pltpu.CompilerParams(
            collective_id=0, has_side_effects=True, vmem_limit_bytes=40 << 20),
        name="exchange",
    )(
        pltpu.with_memory_space_constraint(band_bins.reshape(groups, group), pltpu.HBM),
        pltpu.with_memory_space_constraint(traces, pltpu.HBM),
    )

    return pl.pallas_call(
        place_kernel,
        out_shape=jax.ShapeDtypeStruct((1, 4, bins, 2, channels, channels), jnp.bfloat16),
        in_specs=[pl.BlockSpec(memory_space=pltpu.SMEM), pl.BlockSpec(memory_space=pl.ANY)]
        + [pl.BlockSpec(memory_space=pltpu.VMEM)] * 3,
        out_specs=pl.BlockSpec(memory_space=pl.ANY),
        scratch_shapes=[
            pltpu.SMEM((1, 4), jnp.int32),
            pltpu.VMEM((bins, 2, channels, channels), jnp.bfloat16),
            pltpu.VMEM((bins // 4, 2, channels, channels), jnp.bfloat16),
            pltpu.SemaphoreType.DMA,
            pltpu.SemaphoreType.DMA,
        ],
        compiler_params=pltpu.CompilerParams(vmem_limit_bytes=40 << 20),
        name="place",
    )(
        partner_counts,
        pltpu.with_memory_space_constraint(partners, pltpu.HBM),
        made, left, last,
    )


def solution(mesh):
    placed = (P("tm", None, "chan"), P(), P("chan", None), P("chan"))
    return jax.shard_map(
        body,
        mesh=mesh,
        in_specs=placed,
        out_specs=P("chan", None, "tm", None, None, None),
        check_vma=False,
    )
```

```python
import functools
import math

import jax
import jax.numpy as jnp
from jax import lax
from jax.experimental import pallas as pl
from jax.experimental.pallas import tpu as pltpu
from jax.sharding import PartitionSpec as P

LANES = 128
MESH = pl.DeviceIdType.MESH


def unit_circle(turns_number, samples):
    quarter = samples // 4
    quadrant = jnp.floor(turns_number * (1.0 / quarter) + 0.5)
    x = (turns_number - quadrant * quarter) * (math.pi / 2 / quarter)
    y = x * x
    sine = x * (1 + y * (-1 / 6 + y * (1 / 120 + y * (-1 / 5040 + y * (1 / 362880)))))
    cosine = 1 + y * (-1 / 2 + y * (1 / 24 + y * (-1 / 720 + y * (1 / 40320 + y * (-1 / 3628800)))))
    which = quadrant.astype(jnp.int32)
    odd = (which & 1) == 1
    c = jnp.where(odd, sine, cosine)
    s = jnp.where(odd, cosine, sine)
    c = jnp.where(((which + 1) & 2) == 2, -c, c)
    s = jnp.where((which & 2) == 2, -s, s)
    return c, s


def exchange_kernel(tm_count, bins_hbm, traces_hbm, partners_hbm, made_ref, left_ref, last_ref, partners_ref, bins_ref, traces_ref, table_ref, spectra_ref,
                    send_ref, held, upper, lower, second, wide, block_ref, early, early_second, load_sem, out_sem, in_sem,
                    down_send, down_recv, up_send, up_recv, relay_send, relay_recv, early_send, early_recv, again_send, again_recv):
    me = lax.axis_index("tm")
    block = lax.axis_index("chan")
    blocks = lax.axis_size("chan")
    has_below = block > 0
    has_above = block < blocks - 1
    windows, samples, channels = traces_ref.shape
    groups, group = bins_ref.shape
    bin_count = groups * group
    rows = send_ref.shape[1]
    chips = tm_count // 2
    side = math.isqrt(chips)
    chip = me // 2
    core = lax.rem(me, 2)
    chip_y = chip // side
    chip_x = lax.rem(chip, side)

    barrier = pltpu.get_barrier_semaphore()

    load_bins = pltpu.make_async_copy(bins_hbm, bins_ref, load_sem.at[0])
    load_traces = pltpu.make_async_copy(traces_hbm, traces_ref, load_sem.at[1])
    load_bins.start()
    load_traces.start()
    load_partners = pltpu.make_async_copy(partners_hbm, partners_ref, load_sem.at[2])
    load_partners.start()

    @pl.loop(1, tm_count)
    def _(r):
        pl.semaphore_signal(barrier, inc=1, device_id=(block, lax.rem(me + r, tm_count)), device_id_type=MESH)

    @pl.when(has_below)
    def _():
        pl.semaphore_signal(barrier, inc=1, device_id=(block - 1, me), device_id_type=MESH)

    @pl.when(has_above)
    def _():
        pl.semaphore_signal(barrier, inc=1, device_id=(block + 1, me), device_id_type=MESH)

    lane = lax.broadcasted_iota(jnp.int32, (group, LANES), 1).astype(jnp.float32)
    load_bins.wait()
    power = jnp.zeros((1, windows * channels), jnp.float32)
    for g in range(groups):
        row = bins_ref[g : g + 1, :].astype(jnp.float32)
        number = jnp.broadcast_to(row, (group, group)).T
        c, s = unit_circle(number * lane, samples)
        step_c, step_s = unit_circle(number * float(LANES), samples)
        for q in range(samples // LANES):
            table_ref[g % 2, :group, q * LANES : (q + 1) * LANES] = c.astype(jnp.bfloat16)
            table_ref[g % 2, group:, q * LANES : (q + 1) * LANES] = (-s).astype(jnp.bfloat16)
            c, s = c * step_c - s * step_s, s * step_c + c * step_s
        if g == 0:
            load_traces.wait()
        both = jnp.concatenate([traces_ref[w] for w in range(windows)], axis=1)
        y = jnp.dot(table_ref[g % 2], both, preferred_element_type=jnp.float32)
        spectra_ref[g] = y
        power = power + jnp.sum(y * y, axis=0, keepdims=True)
    scale = lax.rsqrt(power * (1.0 / (2 * bin_count)) + 1e-06)
    per = group // 16
    for g in range(groups):
        y = (spectra_ref[g] * scale).reshape(2, per, 2, 8, windows * channels)
        parts = []
        for w in range(windows):
            for h in range(2):
                for p in range(2):
                    parts.append(y[p, :, h, :, w * channels : (w + 1) * channels])
        send_ref[g * per : (g + 1) * per] = jnp.concatenate(parts, axis=1).astype(jnp.bfloat16)

    others = has_below.astype(jnp.int32) + has_above.astype(jnp.int32)
    pl.semaphore_wait(barrier, tm_count - 1 + others)

    def fold(d):
        return d + d // 2 - 2 * (d // 3)

    def chip_at(step, sign):
        dy, dx = fold(step // side), fold(lax.rem(step, side))
        return lax.rem(chip_y + sign * dy + side, side) * side + lax.rem(chip_x + sign * dx + side, side)

    def spread(to):
        pltpu.make_async_remote_copy(
            src_ref=send_ref.at[to], dst_ref=held.at[me],
            send_sem=out_sem, recv_sem=in_sem.at[chip],
            device_id=(block, to), device_id_type=MESH).start()

    def pair(ref, f):
        return ref.at[pl.ds(f * 2, 2)]

    plain = rows - rows // windows

    def first_part(ref, f):
        return ref.at[pl.ds(f * 2, 2), pl.ds(0, plain)]

    def early_down(hop):
        return pltpu.make_async_remote_copy(
            src_ref=early if hop else send_ref.at[:, pl.ds(plain, rows - plain)],
            dst_ref=early_second if hop else early,
            send_sem=early_send.at[hop], recv_sem=early_recv.at[hop],
            device_id=(block - 1, me), device_id_type=MESH)

    def spread_again(hop, ref, to_ref):
        def one(to):
            pltpu.make_async_remote_copy(
                src_ref=ref.at[to], dst_ref=to_ref.at[me, pl.ds(plain, rows - plain)],
                send_sem=again_send.at[hop], recv_sem=again_recv.at[hop],
                device_id=(block, to), device_id_type=MESH).start()

        one(chip * 2 + 1 - core)

        @pl.loop(1, chips)
        def _(step):
            to = chip_at(step, 1)
            one(to * 2 + core)
            one(to * 2 + 1 - core)

        to_ref[me, plain:rows, :] = ref[me]

    def down(f):
        return pltpu.make_async_remote_copy(
            src_ref=first_part(held, f), dst_ref=first_part(upper, f), send_sem=down_send, recv_sem=down_recv.at[f],
            device_id=(block - 1, me), device_id_type=MESH)

    def up(f):
        return pltpu.make_async_remote_copy(
            src_ref=pair(held, f), dst_ref=pair(lower, f), send_sem=up_send, recv_sem=up_recv,
            device_id=(block + 1, me), device_id_type=MESH)

    def relay(f):
        return pltpu.make_async_remote_copy(
            src_ref=first_part(upper, f), dst_ref=first_part(second, f), send_sem=relay_send, recv_sem=relay_recv,
            device_id=(block - 1, me), device_id_type=MESH)

    def forward(f):
        @pl.when(has_below)
        def _():
            down(f).start()

        @pl.when(has_above)
        def _():
            up(f).start()

    def wait_for(ref, sem):
        pltpu.make_async_copy(ref, ref, sem).wait()

    @pl.when(has_below)
    def _():
        early_down(0).start()

    spread(chip * 2 + 1 - core)

    @pl.loop(1, chips)
    def _(step):
        to = chip_at(step, 1)
        spread(to * 2 + core)
        spread(to * 2 + 1 - core)

    held[me] = send_ref[me]
    wait_for(held.at[0], in_sem.at[chip])
    forward(chip)

    @pl.loop(1, chips)
    def _(step):
        f = chip_at(step, -1)
        wait_for(pair(held, 0), in_sem.at[f])
        forward(f)

    total = tm_count * windows

    def regroup(ref, to_ref):
        wide[...] = ref[...].astype(jnp.float32).reshape(tm_count * rows, channels)
        for j in range(16):
            for p in range(2):
                lines = wide[pl.ds(j // 8 * 16 + p * 8 + j % 8, total, stride=32), :]
                to_ref[j, p * total : (p + 1) * total, :] = lines.astype(jnp.bfloat16)

    def products(where):
        @pl.loop(0, 16)
        def _(j):
            both = jnp.dot(left_ref[j], block_ref[j], preferred_element_type=jnp.float32)
            made_ref[where, j] = both.astype(jnp.bfloat16).reshape(2, channels, channels)

    @pl.when(has_above)
    def _():
        early_down(0).wait_recv()

        @pl.when(has_below)
        def _():
            early_down(1).start()

        spread_again(0, early, upper)

    regroup(held, block_ref)

    @pl.loop(0, 16)
    def _(j):
        own = block_ref[j]
        left_ref[j, :channels, :] = own.T
        left_ref[j, channels:, :] = jnp.concatenate([own[total:], -own[:total]], axis=0).T

    products(0)

    @pl.when(has_above)
    def _():
        @pl.loop(0, chips)
        def _(step):
            f = chip_at(step, -1)
            wait_for(first_part(upper, 0), down_recv.at[f])

            @pl.when(has_below)
            def _():
                relay(f).start()

    @pl.when(has_above)
    def _():
        wait_for(early.at[pl.ds(0, tm_count - 1)], again_recv.at[0])
        regroup(upper, block_ref)
        products(1)

    @pl.when(block < blocks - 2)
    def _():
        early_down(1).wait_recv()
        spread_again(1, early_second, second)

    @pl.when(has_below)
    def _():
        wait_for(lower, up_recv)
        regroup(lower, block_ref)
        products(2)

    wait_for(held.at[pl.ds(0, tm_count - 1)], out_sem)

    load_partners.wait()
    last_window = early.at[pl.ds(0, tm_count - 1)]

    @pl.when(has_below)
    def _():
        early_down(0).wait_send()
        wait_for(held.at[:, pl.ds(0, plain)], down_send)

    @pl.when(has_above)
    def _():
        wait_for(held, up_send)
        wait_for(last_window, again_send.at[0])

    @pl.when(has_above & has_below)
    def _():
        early_down(1).wait_send()
        wait_for(held.at[:, pl.ds(0, plain)], relay_send)

    @pl.when(block < blocks - 2)
    def _():
        wait_for(last_window, again_send.at[1])
        wait_for(last_window, again_recv.at[1])
        wait_for(second.at[:, pl.ds(0, plain)], relay_recv)
        regroup(second, last_ref)


def place_kernel(counts_ref, partners_ref, made_ref, left_ref, last_ref, out_hbm,
                 product_ref, zero_ref, out_sem):
    block = lax.axis_index("chan")
    bins, _, channels = last_ref.shape
    slots = out_hbm.shape[1]
    pltpu.make_async_copy(made_ref.at[0], out_hbm.at[0, 0], out_sem).start()
    slot_number = lax.broadcasted_iota(jnp.int32, partners_ref.shape, 1)
    offsets = [None]
    for slot in range(1, slots):
        offsets.append(jnp.sum(jnp.where(slot_number == slot, partners_ref[...], 0)) - block)
    zero_ref[...] = jnp.zeros_like(zero_ref)
    for slot in range(1, slots):
        offset = offsets[slot]
        listed = slot < counts_ref[0]

        @pl.when(listed & (offset == 1))
        def _():
            pltpu.make_async_copy(made_ref.at[1], out_hbm.at[0, slot], out_sem).start()

        @pl.when(listed & (offset == -1))
        def _():
            pltpu.make_async_copy(made_ref.at[2], out_hbm.at[0, slot], out_sem).start()

        @pl.when(jnp.logical_not(listed))
        def _():
            for k in range(0, bins, zero_ref.shape[0]):
                to = out_hbm.at[0, slot, pl.ds(k, zero_ref.shape[0])]
                pltpu.make_async_copy(zero_ref, to, out_sem).start()

    for slot in range(1, slots):
        @pl.when((slot < counts_ref[0]) & (offsets[slot] == 2))
        def _():
            for k in range(bins):
                both = jnp.dot(left_ref[k], last_ref[k], preferred_element_type=jnp.float32)
                product_ref[k] = both.astype(jnp.bfloat16).reshape(2, channels, channels)
                if k % 2 == 1:
                    part = pl.ds(k - 1, 2)
                    pltpu.make_async_copy(product_ref.at[part], out_hbm.at[0, slot, part], out_sem).start()

    for slot in range(slots):
        pltpu.make_async_copy(made_ref.at[0], out_hbm.at[0, slot], out_sem).wait()


def body(traces, band_bins, partners, partner_counts):
    windows, samples, channels = traces.shape
    bin_count = band_bins.shape[0]
    tm_count = lax.axis_size("tm")
    group = min(128, bin_count)
    groups = bin_count // group
    bins = bin_count // tm_count
    rows = 32 * windows
    chips = tm_count // 2
    depth = 2 * windows * tm_count
    dma = pltpu.SemaphoreType.DMA
    buffer = pltpu.VMEM((tm_count, rows, channels), jnp.bfloat16)
    made, left, last, listed = pl.pallas_call(
        functools.partial(exchange_kernel, tm_count),
        out_shape=[
            pltpu.VMEM((3, bins, 2, channels, channels), jnp.bfloat16),
            pltpu.VMEM((bins, 2 * channels, depth), jnp.bfloat16),
            pltpu.VMEM((bins, depth, channels), jnp.bfloat16),
            pltpu.VMEM(partners.shape, jnp.int32),
        ],
        in_specs=[pl.BlockSpec(memory_space=pltpu.HBM)] * 3,
        out_specs=[pl.BlockSpec(memory_space=pltpu.VMEM)] * 4,
        scratch_shapes=[
            pltpu.VMEM((groups, group), jnp.int32),
            pltpu.VMEM((windows, samples, channels), jnp.bfloat16),
            pltpu.VMEM((2, 2 * group, samples), jnp.bfloat16),
            pltpu.VMEM((groups, 2 * group, windows * channels), jnp.float32),
            buffer, buffer, buffer, buffer, buffer,
            pltpu.VMEM((tm_count * rows, channels), jnp.float32),
            pltpu.VMEM((bins, depth, channels), jnp.bfloat16),
            pltpu.VMEM((tm_count, rows // windows, channels), jnp.bfloat16),
            pltpu.VMEM((tm_count, rows // windows, channels), jnp.bfloat16),
            dma((3,)), dma, dma((chips,)),
            dma, dma((chips,)), dma, dma, dma, dma,
            dma((2,)), dma((2,)), dma((2,)), dma((2,)),
        ],
        compiler_params=pltpu.CompilerParams(
            collective_id=0, has_side_effects=True, vmem_limit_bytes=40 << 20),
        name="exchange",
    )(
        pltpu.with_memory_space_constraint(band_bins.reshape(groups, group), pltpu.HBM),
        pltpu.with_memory_space_constraint(traces, pltpu.HBM),
        pltpu.with_memory_space_constraint(partners, pltpu.HBM),
    )

    return pl.pallas_call(
        place_kernel,
        out_shape=jax.ShapeDtypeStruct((1, 4, bins, 2, channels, channels), jnp.bfloat16),
        in_specs=[pl.BlockSpec(memory_space=pltpu.SMEM)] + [pl.BlockSpec(memory_space=pltpu.VMEM)] * 4,
        out_specs=pl.BlockSpec(memory_space=pl.ANY),
        scratch_shapes=[
            pltpu.VMEM((bins, 2, channels, channels), jnp.bfloat16),
            pltpu.VMEM((bins // 4, 2, channels, channels), jnp.bfloat16),
            pltpu.SemaphoreType.DMA,
        ],
        compiler_params=pltpu.CompilerParams(vmem_limit_bytes=40 << 20),
        name="place",
    )(
        partner_counts, listed, made, left, last,
    )


def solution(mesh):
    placed = (P("tm", None, "chan"), P(), P("chan", None), P("chan"))
    return jax.shard_map(
        body,
        mesh=mesh,
        in_specs=placed,
        out_specs=P("chan", None, "tm", None, None, None),
        check_vma=False,
    )
```

```python
import functools
import math

import jax
import jax.numpy as jnp
from jax import lax
from jax.experimental import pallas as pl
from jax.experimental.pallas import tpu as pltpu
from jax.sharding import PartitionSpec as P

LANES = 128
MESH = pl.DeviceIdType.MESH


def unit_circle(turns_number, samples):
    quarter = samples // 4
    quadrant = jnp.floor(turns_number * (1.0 / quarter) + 0.5)
    x = (turns_number - quadrant * quarter) * (math.pi / 2 / quarter)
    y = x * x
    sine = x * (1 + y * (-1 / 6 + y * (1 / 120 + y * (-1 / 5040 + y * (1 / 362880)))))
    cosine = 1 + y * (-1 / 2 + y * (1 / 24 + y * (-1 / 720 + y * (1 / 40320 + y * (-1 / 3628800)))))
    which = quadrant.astype(jnp.int32)
    odd = (which & 1) == 1
    c = jnp.where(odd, sine, cosine)
    s = jnp.where(odd, cosine, sine)
    c = jnp.where(((which + 1) & 2) == 2, -c, c)
    s = jnp.where((which & 2) == 2, -s, s)
    return c, s


def exchange_kernel(tm_count, bins_hbm, traces_hbm, partners_hbm, made_ref, left_ref, last_ref, partners_ref, bins_ref, traces_ref, table_ref, spectra_ref,
                    send_ref, held, upper, lower, second, wide, block_ref, early, early_second, load_sem, out_sem, in_sem,
                    down_send, down_recv, up_send, up_recv, relay_send, relay_recv, early_send, early_recv, again_send, again_recv):
    me = lax.axis_index("tm")
    block = lax.axis_index("chan")
    blocks = lax.axis_size("chan")
    has_below = block > 0
    has_above = block < blocks - 1
    windows, samples, channels = traces_ref.shape
    groups, group = bins_ref.shape
    bin_count = groups * group
    rows = send_ref.shape[1]
    chips = tm_count // 2
    side = math.isqrt(chips)
    chip = me // 2
    core = lax.rem(me, 2)
    chip_y = chip // side
    chip_x = lax.rem(chip, side)

    barrier = pltpu.get_barrier_semaphore()

    load_bins = pltpu.make_async_copy(bins_hbm, bins_ref, load_sem.at[0])
    load_traces = pltpu.make_async_copy(traces_hbm, traces_ref, load_sem.at[1])
    load_bins.start()
    load_traces.start()
    load_partners = pltpu.make_async_copy(partners_hbm, partners_ref, load_sem.at[2])
    load_partners.start()

    @pl.loop(1, tm_count)
    def _(r):
        pl.semaphore_signal(barrier, inc=1, device_id=(block, lax.rem(me + r, tm_count)), device_id_type=MESH)

    @pl.when(has_below)
    def _():
        pl.semaphore_signal(barrier, inc=1, device_id=(block - 1, me), device_id_type=MESH)

    @pl.when(has_above)
    def _():
        pl.semaphore_signal(barrier, inc=1, device_id=(block + 1, me), device_id_type=MESH)

    lane = lax.broadcasted_iota(jnp.int32, (group, LANES), 1).astype(jnp.float32)
    load_bins.wait()
    power = jnp.zeros((1, windows * channels), jnp.float32)
    half = samples // 2
    for g in range(groups):
        row = bins_ref[g : g + 1, :].astype(jnp.float32)
        number = jnp.broadcast_to(row, (group, group)).T
        sign = 1 - 2 * (number - 2 * jnp.floor(number * 0.5))
        c, s = unit_circle(number * lane, samples)
        step_c, step_s = unit_circle(number * float(LANES), samples)
        s, step_s = -s, -step_s
        for first in range(0, half, LANES):
            n = min(LANES, half - first)
            table_ref[g % 2, :group, first : first + n] = c[:, :n].astype(jnp.bfloat16)
            table_ref[g % 2, group:, first : first + n] = s[:, :n].astype(jnp.bfloat16)
            c, s = c * step_c - s * step_s, s * step_c + c * step_s
        if g == 0:
            load_traces.wait()
        halves = [traces_ref[w, i * half : (i + 1) * half] for i in range(2) for w in range(windows)]
        y = jnp.dot(table_ref[g % 2], jnp.concatenate(halves, axis=1), preferred_element_type=jnp.float32)
        signs = jnp.concatenate([jnp.concatenate([sign] * windows, axis=1)] * 2, axis=0)
        y = y[:, : windows * channels] + signs * y[:, windows * channels :]
        spectra_ref[g] = y
        power = power + jnp.sum(y * y, axis=0, keepdims=True)
    scale = lax.rsqrt(power * (1.0 / (2 * bin_count)) + 1e-06)
    per = group // 16
    for g in range(groups):
        y = (spectra_ref[g] * scale).reshape(2, per, 2, 8, windows * channels)
        parts = []
        for w in range(windows):
            for h in range(2):
                for p in range(2):
                    parts.append(y[p, :, h, :, w * channels : (w + 1) * channels])
        send_ref[g * per : (g + 1) * per] = jnp.concatenate(parts, axis=1).astype(jnp.bfloat16)

    others = has_below.astype(jnp.int32) + has_above.astype(jnp.int32)
    pl.semaphore_wait(barrier, tm_count - 1 + others)

    def fold(d):
        return d + d // 2 - 2 * (d // 3)

    def chip_at(step, sign):
        dy, dx = fold(step // side), fold(lax.rem(step, side))
        return lax.rem(chip_y + sign * dy + side, side) * side + lax.rem(chip_x + sign * dx + side, side)

    def spread(to):
        pltpu.make_async_remote_copy(
            src_ref=send_ref.at[to], dst_ref=held.at[me],
            send_sem=out_sem, recv_sem=in_sem.at[chip],
            device_id=(block, to), device_id_type=MESH).start()

    def pair(ref, f):
        return ref.at[pl.ds(f * 2, 2)]

    plain = rows - rows // windows

    def first_part(ref, f):
        return ref.at[pl.ds(f * 2, 2), pl.ds(0, plain)]

    def early_down(hop):
        return pltpu.make_async_remote_copy(
            src_ref=early if hop else send_ref.at[:, pl.ds(plain, rows - plain)],
            dst_ref=early_second if hop else early,
            send_sem=early_send.at[hop], recv_sem=early_recv.at[hop],
            device_id=(block - 1, me), device_id_type=MESH)

    def spread_again(hop, ref, to_ref):
        def one(to):
            pltpu.make_async_remote_copy(
                src_ref=ref.at[to], dst_ref=to_ref.at[me, pl.ds(plain, rows - plain)],
                send_sem=again_send.at[hop], recv_sem=again_recv.at[hop],
                device_id=(block, to), device_id_type=MESH).start()

        one(chip * 2 + 1 - core)

        @pl.loop(1, chips)
        def _(step):
            to = chip_at(step, 1)
            one(to * 2 + core)
            one(to * 2 + 1 - core)

        to_ref[me, plain:rows, :] = ref[me]

    def down(f):
        return pltpu.make_async_remote_copy(
            src_ref=first_part(held, f), dst_ref=first_part(upper, f), send_sem=down_send, recv_sem=down_recv.at[f],
            device_id=(block - 1, me), device_id_type=MESH)

    def up(f):
        return pltpu.make_async_remote_copy(
            src_ref=pair(held, f), dst_ref=pair(lower, f), send_sem=up_send, recv_sem=up_recv,
            device_id=(block + 1, me), device_id_type=MESH)

    def relay(f):
        return pltpu.make_async_remote_copy(
            src_ref=first_part(upper, f), dst_ref=first_part(second, f), send_sem=relay_send, recv_sem=relay_recv,
            device_id=(block - 1, me), device_id_type=MESH)

    def forward(f):
        @pl.when(has_below)
        def _():
            down(f).start()

        @pl.when(has_above)
        def _():
            up(f).start()

    def wait_for(ref, sem):
        pltpu.make_async_copy(ref, ref, sem).wait()

    @pl.when(has_below)
    def _():
        early_down(0).start()

    spread(chip * 2 + 1 - core)

    @pl.loop(1, chips)
    def _(step):
        to = chip_at(step, 1)
        spread(to * 2 + core)
        spread(to * 2 + 1 - core)

    held[me] = send_ref[me]
    total = tm_count * windows

    def regroup(ref, to_ref, w):
        some = ref[:, w * 32 : (w + 1) * 32, :].astype(jnp.float32)
        wide[...] = some.reshape(tm_count * 32, channels)
        for j in range(16):
            for p in range(2):
                lines = wide[pl.ds(j // 8 * 16 + p * 8 + j % 8, tm_count, stride=32), :]
                at = p * total + w * tm_count
                to_ref[j, at : at + tm_count, :] = lines.astype(jnp.bfloat16)

    def products(where):
        @pl.loop(0, 16, step=4)
        def _(first):
            for j in range(4):
                both = jnp.dot(left_ref[first + j], block_ref[first + j], preferred_element_type=jnp.float32)
                made_ref[where, first + j] = both.astype(jnp.bfloat16).reshape(2, channels, channels)

    def forward_some(first, last):
        @pl.loop(first, last)
        def _(step):
            f = chip_at(step, -1)
            wait_for(pair(held, 0), in_sem.at[f])
            forward(f)

    def relay_some(first, last):
        @pl.loop(first, last)
        def _(step):
            f = chip_at(step, -1)
            wait_for(first_part(upper, 0), down_recv.at[f])

            @pl.when(has_below)
            def _():
                relay(f).start()

    middle = chips // 2
    wait_for(held.at[0], in_sem.at[chip])
    forward(chip)
    forward_some(1, middle)

    @pl.when(has_above)
    def _():
        early_down(0).wait_recv()

        @pl.when(has_below)
        def _():
            early_down(1).start()

    forward_some(middle, chips)

    @pl.when(has_above)
    def _():
        spread_again(0, early, upper)

    for w in range(windows):
        regroup(held, block_ref, w)

    @pl.loop(0, 16)
    def _(j):
        own = block_ref[j]
        left_ref[j, :channels, :] = own.T
        left_ref[j, channels:, :] = jnp.concatenate([own[total:], -own[:total]], axis=0).T

    products(0)

    @pl.when(has_above)
    def _():
        relay_some(0, middle)

    @pl.when(block < blocks - 2)
    def _():
        early_down(1).wait_recv()
        spread_again(1, early_second, second)

    last_window = early.at[pl.ds(0, tm_count - 1)]

    @pl.when(has_above)
    def _():
        relay_some(middle, chips)
        wait_for(last_window, again_recv.at[0])
        for w in range(windows):
            regroup(upper, block_ref, w)
        products(1)

    @pl.when(has_below)
    def _():
        wait_for(lower, up_recv)
        for w in range(windows):
            regroup(lower, block_ref, w)
        products(2)

    wait_for(held.at[pl.ds(0, tm_count - 1)], out_sem)

    load_partners.wait()
    @pl.when(has_below)
    def _():
        early_down(0).wait_send()
        wait_for(held.at[:, pl.ds(0, plain)], down_send)

    @pl.when(has_above)
    def _():
        wait_for(held, up_send)
        wait_for(last_window, again_send.at[0])

    @pl.when(has_above & has_below)
    def _():
        early_down(1).wait_send()
        wait_for(held.at[:, pl.ds(0, plain)], relay_send)

    @pl.when(block < blocks - 2)
    def _():
        wait_for(last_window, again_send.at[1])
        wait_for(last_window, again_recv.at[1])
        for w in range(1, windows):
            regroup(second, last_ref, w)
        wait_for(second.at[:, pl.ds(0, plain)], relay_recv)
        regroup(second, last_ref, 0)


def place_kernel(counts_ref, partners_ref, made_ref, left_ref, last_ref, out_hbm,
                 product_ref, zero_ref, out_sem):
    block = lax.axis_index("chan")
    bins, _, channels = last_ref.shape
    slots = out_hbm.shape[1]
    pltpu.make_async_copy(made_ref.at[0], out_hbm.at[0, 0], out_sem).start()
    slot_number = lax.broadcasted_iota(jnp.int32, partners_ref.shape, 1)
    offsets = [None]
    for slot in range(1, slots):
        offsets.append(jnp.sum(jnp.where(slot_number == slot, partners_ref[...], 0)) - block)
    zero_ref[...] = jnp.zeros_like(zero_ref)
    for slot in range(1, slots):
        offset = offsets[slot]
        listed = slot < counts_ref[0]

        @pl.when(listed & (offset == 1))
        def _():
            pltpu.make_async_copy(made_ref.at[1], out_hbm.at[0, slot], out_sem).start()

        @pl.when(listed & (offset == -1))
        def _():
            pltpu.make_async_copy(made_ref.at[2], out_hbm.at[0, slot], out_sem).start()

        @pl.when(jnp.logical_not(listed))
        def _():
            for k in range(0, bins, zero_ref.shape[0]):
                to = out_hbm.at[0, slot, pl.ds(k, zero_ref.shape[0])]
                pltpu.make_async_copy(zero_ref, to, out_sem).start()

    for slot in range(1, slots):
        @pl.when((slot < counts_ref[0]) & (offsets[slot] == 2))
        def _():
            for k in range(bins):
                both = jnp.dot(left_ref[k], last_ref[k], preferred_element_type=jnp.float32)
                product_ref[k] = both.astype(jnp.bfloat16).reshape(2, channels, channels)
                if k % 2 == 1:
                    part = pl.ds(k - 1, 2)
                    pltpu.make_async_copy(product_ref.at[part], out_hbm.at[0, slot, part], out_sem).start()

    for slot in range(slots):
        pltpu.make_async_copy(made_ref.at[0], out_hbm.at[0, slot], out_sem).wait()


def body(traces, band_bins, partners, partner_counts):
    windows, samples, channels = traces.shape
    bin_count = band_bins.shape[0]
    tm_count = lax.axis_size("tm")
    group = min(128, bin_count)
    groups = bin_count // group
    bins = bin_count // tm_count
    rows = 32 * windows
    chips = tm_count // 2
    depth = 2 * windows * tm_count
    dma = pltpu.SemaphoreType.DMA
    buffer = pltpu.VMEM((tm_count, rows, channels), jnp.bfloat16)
    made, left, last, listed = pl.pallas_call(
        functools.partial(exchange_kernel, tm_count),
        out_shape=[
            pltpu.VMEM((3, bins, 2, channels, channels), jnp.bfloat16),
            pltpu.VMEM((bins, 2 * channels, depth), jnp.bfloat16),
            pltpu.VMEM((bins, depth, channels), jnp.bfloat16),
            pltpu.VMEM(partners.shape, jnp.int32),
        ],
        in_specs=[pl.BlockSpec(memory_space=pltpu.HBM)] * 3,
        out_specs=[pl.BlockSpec(memory_space=pltpu.VMEM)] * 4,
        scratch_shapes=[
            pltpu.VMEM((groups, group), jnp.int32),
            pltpu.VMEM((windows, samples, channels), jnp.bfloat16),
            pltpu.VMEM((2, 2 * group, samples // 2), jnp.bfloat16),
            pltpu.VMEM((groups, 2 * group, windows * channels), jnp.float32),
            buffer, buffer, buffer, buffer, buffer,
            pltpu.VMEM((tm_count * 32, channels), jnp.float32),
            pltpu.VMEM((bins, depth, channels), jnp.bfloat16),
            pltpu.VMEM((tm_count, rows // windows, channels), jnp.bfloat16),
            pltpu.VMEM((tm_count, rows // windows, channels), jnp.bfloat16),
            dma((3,)), dma, dma((chips,)),
            dma, dma((chips,)), dma, dma, dma, dma,
            dma((2,)), dma((2,)), dma((2,)), dma((2,)),
        ],
        compiler_params=pltpu.CompilerParams(
            collective_id=0, has_side_effects=True, vmem_limit_bytes=40 << 20),
        name="exchange",
    )(
        pltpu.with_memory_space_constraint(band_bins.reshape(groups, group), pltpu.HBM),
        pltpu.with_memory_space_constraint(traces, pltpu.HBM),
        pltpu.with_memory_space_constraint(partners, pltpu.HBM),
    )

    return pl.pallas_call(
        place_kernel,
        out_shape=jax.ShapeDtypeStruct((1, 4, bins, 2, channels, channels), jnp.bfloat16),
        in_specs=[pl.BlockSpec(memory_space=pltpu.SMEM)] + [pl.BlockSpec(memory_space=pltpu.VMEM)] * 4,
        out_specs=pl.BlockSpec(memory_space=pl.ANY),
        scratch_shapes=[
            pltpu.VMEM((bins, 2, channels, channels), jnp.bfloat16),
            pltpu.VMEM((bins // 4, 2, channels, channels), jnp.bfloat16),
            pltpu.SemaphoreType.DMA,
        ],
        compiler_params=pltpu.CompilerParams(vmem_limit_bytes=40 << 20),
        name="place",
    )(
        partner_counts, listed, made, left, last,
    )


def solution(mesh):
    placed = (P("tm", None, "chan"), P(), P("chan", None), P("chan"))
    return jax.shard_map(
        body,
        mesh=mesh,
        in_specs=placed,
        out_specs=P("chan", None, "tm", None, None, None),
        check_vma=False,
    )
```

```python
import functools
import math

import jax
import jax.numpy as jnp
from jax import lax
from jax.experimental import pallas as pl
from jax.experimental.pallas import tpu as pltpu
from jax.sharding import PartitionSpec as P

LANES = 128
MESH = pl.DeviceIdType.MESH


def unit_circle(turns_number, samples):
    quarter = samples // 4
    quadrant = jnp.floor(turns_number * (1.0 / quarter) + 0.5)
    x = (turns_number - quadrant * quarter) * (math.pi / 2 / quarter)
    y = x * x
    sine = x * (1 + y * (-1 / 6 + y * (1 / 120 + y * (-1 / 5040 + y * (1 / 362880)))))
    cosine = 1 + y * (-1 / 2 + y * (1 / 24 + y * (-1 / 720 + y * (1 / 40320 + y * (-1 / 3628800)))))
    which = quadrant.astype(jnp.int32)
    odd = (which & 1) == 1
    c = jnp.where(odd, sine, cosine)
    s = jnp.where(odd, cosine, sine)
    c = jnp.where(((which + 1) & 2) == 2, -c, c)
    s = jnp.where((which & 2) == 2, -s, s)
    return c, s


def exchange_kernel(tm_count, bins_hbm, traces_hbm, partners_hbm, made_ref, left_ref, last_ref, partners_ref, bins_ref, traces_ref, table_ref, spectra_ref,
                    send_ref, held, upper, lower, second, wide, block_ref, early, early_second, load_sem, out_sem, in_sem,
                    down_send, down_recv, up_send, up_recv, relay_send, relay_recv, early_send, early_recv, again_send, again_recv):
    me = lax.axis_index("tm")
    block = lax.axis_index("chan")
    blocks = lax.axis_size("chan")
    has_below = block > 0
    has_above = block < blocks - 1
    windows, samples, channels = traces_ref.shape
    groups, group = bins_ref.shape
    bin_count = groups * group
    rows = send_ref.shape[1]
    chips = tm_count // 2
    side = math.isqrt(chips)
    chip = me // 2
    core = lax.rem(me, 2)
    chip_y = chip // side
    chip_x = lax.rem(chip, side)

    barrier = pltpu.get_barrier_semaphore()

    load_bins = pltpu.make_async_copy(bins_hbm, bins_ref, load_sem.at[0])
    load_traces = pltpu.make_async_copy(traces_hbm, traces_ref, load_sem.at[1])
    load_bins.start()
    load_partners = pltpu.make_async_copy(partners_hbm, partners_ref, load_sem.at[2])

    @pl.when(has_below)
    def _():
        pl.semaphore_signal(barrier, inc=1, device_id=(block - 1, me), device_id_type=MESH)

    @pl.when(has_above)
    def _():
        pl.semaphore_signal(barrier, inc=1, device_id=(block + 1, me), device_id_type=MESH)

    for r in range(1, tm_count):
        pl.semaphore_signal(barrier, inc=1, device_id=(block, lax.rem(me + r, tm_count)), device_id_type=MESH)

    load_traces.start()
    load_partners.start()

    lane = lax.broadcasted_iota(jnp.int32, (group, LANES), 1).astype(jnp.float32)
    load_bins.wait()
    power = jnp.zeros((1, windows * channels), jnp.float32)
    half = samples // 2
    for g in range(groups):
        row = bins_ref[g : g + 1, :].astype(jnp.float32)
        number = jnp.broadcast_to(row, (group, group)).T
        sign = 1 - 2 * (number - 2 * jnp.floor(number * 0.5))
        c, s = unit_circle(number * lane, samples)
        s = -s
        half_c = jnp.broadcast_to(c[:, LANES // 2 : LANES // 2 + 1], c.shape)
        half_s = jnp.broadcast_to(s[:, LANES // 2 : LANES // 2 + 1], s.shape)
        step_c, step_s = half_c * half_c - half_s * half_s, 2 * half_c * half_s
        for first in range(0, half, LANES):
            n = min(LANES, half - first)
            table_ref[g % 2, :group, first : first + n] = c[:, :n].astype(jnp.bfloat16)
            table_ref[g % 2, group:, first : first + n] = s[:, :n].astype(jnp.bfloat16)
            c, s = c * step_c - s * step_s, s * step_c + c * step_s
        if g == 0:
            load_traces.wait()
        halves = [traces_ref[w, i * half : (i + 1) * half] for i in range(2) for w in range(windows)]
        y = jnp.dot(table_ref[g % 2], jnp.concatenate(halves, axis=1), preferred_element_type=jnp.float32)
        signs = jnp.concatenate([jnp.concatenate([sign] * windows, axis=1)] * 2, axis=0)
        y = y[:, : windows * channels] + signs * y[:, windows * channels :]
        spectra_ref[g] = y
        power = power + jnp.sum(y * y, axis=0, keepdims=True)
    scale = lax.rsqrt(power * (1.0 / (2 * bin_count)) + 1e-06)
    per = group // 16

    def whiten(w):
        at = slice(w * channels, (w + 1) * channels)
        for g in range(groups):
            y = (spectra_ref[g][:, at] * scale[:, at]).reshape(2, per, 2, 8, channels)
            parts = [y[p, :, h] for h in range(2) for p in range(2)]
            send_ref[g * per : (g + 1) * per, w * 32 : (w + 1) * 32, :] = jnp.concatenate(parts, axis=1).astype(jnp.bfloat16)

    for w in range(1, windows):
        whiten(w)

    others = has_below.astype(jnp.int32) + has_above.astype(jnp.int32)
    pl.semaphore_wait(barrier, tm_count - 1 + others)

    turns = sorted(
        ((dy, dx) for dy in range(side) for dx in range(side)),
        key=lambda at: (min(at[0], side - at[0]) + min(at[1], side - at[1]), max(at), at),
    )

    def chip_at(step, sign):
        dy, dx = turns[step]
        return lax.rem(chip_y + sign * dy + side, side) * side + lax.rem(chip_x + sign * dx + side, side)

    def spread(to):
        pltpu.make_async_remote_copy(
            src_ref=send_ref.at[to], dst_ref=held.at[me],
            send_sem=out_sem, recv_sem=in_sem.at[chip],
            device_id=(block, to), device_id_type=MESH).start()

    def pair(ref, f):
        return ref.at[pl.ds(f * 2, 2)]

    plain = rows - rows // windows

    def first_part(ref, f):
        return ref.at[pl.ds(f * 2, 2), pl.ds(0, plain)]

    def early_down(hop):
        return pltpu.make_async_remote_copy(
            src_ref=early if hop else send_ref.at[:, pl.ds(plain, rows - plain)],
            dst_ref=early_second if hop else early,
            send_sem=early_send.at[hop], recv_sem=early_recv.at[hop],
            device_id=(block - 1, me), device_id_type=MESH)

    def spread_again(hop, ref, to_ref):
        def one(to):
            pltpu.make_async_remote_copy(
                src_ref=ref.at[to], dst_ref=to_ref.at[me, pl.ds(plain, rows - plain)],
                send_sem=again_send.at[hop], recv_sem=again_recv.at[hop],
                device_id=(block, to), device_id_type=MESH).start()

        one(chip * 2 + 1 - core)

        for step in range(1, chips):
            to = chip_at(step, 1)
            one(to * 2 + core)
            one(to * 2 + 1 - core)

        to_ref[me, plain:rows, :] = ref[me]

    def down(f):
        return pltpu.make_async_remote_copy(
            src_ref=first_part(held, f), dst_ref=first_part(upper, f), send_sem=down_send, recv_sem=down_recv.at[f],
            device_id=(block - 1, me), device_id_type=MESH)

    def up(f):
        return pltpu.make_async_remote_copy(
            src_ref=pair(held, f), dst_ref=pair(lower, f), send_sem=up_send, recv_sem=up_recv,
            device_id=(block + 1, me), device_id_type=MESH)

    def relay(f):
        return pltpu.make_async_remote_copy(
            src_ref=first_part(upper, f), dst_ref=first_part(second, f), send_sem=relay_send, recv_sem=relay_recv,
            device_id=(block - 1, me), device_id_type=MESH)

    def forward(f):
        @pl.when(has_below)
        def _():
            down(f).start()

        @pl.when(has_above)
        def _():
            up(f).start()

    def wait_for(ref, sem):
        pltpu.make_async_copy(ref, ref, sem).wait()

    @pl.when(has_below)
    def _():
        early_down(0).start()

    whiten(0)
    spread(chip * 2 + 1 - core)

    for step in range(1, chips):
        to = chip_at(step, 1)
        spread(to * 2 + core)
        spread(to * 2 + 1 - core)

    held[me] = send_ref[me]
    total = tm_count * windows

    def regroup(ref, to_ref, w):
        some = ref[:, w * 32 : (w + 1) * 32, :].astype(jnp.float32)
        wide[...] = some.reshape(tm_count * 32, channels)
        for j in range(16):
            for p in range(2):
                lines = wide[pl.ds(j // 8 * 16 + p * 8 + j % 8, tm_count, stride=32), :]
                at = p * total + w * tm_count
                to_ref[j, at : at + tm_count, :] = lines.astype(jnp.bfloat16)

    def products(where):
        @pl.loop(0, 16, step=4)
        def _(first):
            for j in range(4):
                both = jnp.dot(left_ref[first + j], block_ref[first + j], preferred_element_type=jnp.float32)
                made_ref[where, first + j] = both.astype(jnp.bfloat16).reshape(2, channels, channels)

    def forward_some(first, last):
        for step in range(first, last):
            f = chip_at(step, -1)
            wait_for(pair(held, 0), in_sem.at[f])
            forward(f)

    def relay_some(first, last):
        for step in range(first, last):
            f = chip_at(step, -1)
            wait_for(first_part(upper, 0), down_recv.at[f])

            @pl.when(has_below)
            def _():
                relay(f).start()

    middle = chips // 2
    wait_for(held.at[0], in_sem.at[chip])
    forward(chip)
    forward_some(1, middle)

    @pl.when(has_above)
    def _():
        early_down(0).wait_recv()

        @pl.when(has_below)
        def _():
            early_down(1).start()

    forward_some(middle, chips)

    @pl.when(has_above)
    def _():
        spread_again(0, early, upper)

    for w in range(windows):
        regroup(held, block_ref, w)

    @pl.loop(0, 16)
    def _(j):
        own = block_ref[j]
        left_ref[j, :channels, :] = own.T
        left_ref[j, channels:, :] = jnp.concatenate([own[total:], -own[:total]], axis=0).T

    products(0)

    @pl.when(has_above)
    def _():
        relay_some(0, middle)

    @pl.when(block < blocks - 2)
    def _():
        early_down(1).wait_recv()
        spread_again(1, early_second, second)

    last_window = early.at[pl.ds(0, tm_count - 1)]

    @pl.when(has_above)
    def _():
        relay_some(middle, chips)
        wait_for(last_window, again_recv.at[0])
        for w in range(windows):
            regroup(upper, block_ref, w)
        products(1)

    @pl.when(has_below)
    def _():
        wait_for(lower, up_recv)
        for w in range(windows):
            regroup(lower, block_ref, w)
        products(2)

    wait_for(held.at[pl.ds(0, tm_count - 1)], out_sem)

    load_partners.wait()
    @pl.when(has_below)
    def _():
        early_down(0).wait_send()
        wait_for(held.at[:, pl.ds(0, plain)], down_send)

    @pl.when(has_above)
    def _():
        wait_for(held, up_send)
        wait_for(last_window, again_send.at[0])

    @pl.when(has_above & has_below)
    def _():
        early_down(1).wait_send()
        wait_for(held.at[:, pl.ds(0, plain)], relay_send)

    @pl.when(block < blocks - 2)
    def _():
        wait_for(last_window, again_send.at[1])
        wait_for(last_window, again_recv.at[1])
        for w in range(1, windows):
            regroup(second, last_ref, w)
        wait_for(second.at[:, pl.ds(0, plain)], relay_recv)
        regroup(second, last_ref, 0)


def place_kernel(counts_ref, partners_ref, made_ref, left_ref, last_ref, out_hbm,
                 product_ref, zero_ref, out_sem):
    block = lax.axis_index("chan")
    bins, _, channels = last_ref.shape
    slots = out_hbm.shape[1]
    def put(where, slot):
        for k in range(0, bins, bins // 4):
            part = pl.ds(k, bins // 4)
            pltpu.make_async_copy(made_ref.at[where, part], out_hbm.at[0, slot, part], out_sem).start()

    put(0, 0)
    slot_number = lax.broadcasted_iota(jnp.int32, partners_ref.shape, 1)
    offsets = [None]
    for slot in range(1, slots):
        offsets.append(jnp.sum(jnp.where(slot_number == slot, partners_ref[...], 0)) - block)
    zero_ref[...] = jnp.zeros_like(zero_ref)
    for slot in range(1, slots):
        offset = offsets[slot]
        listed = slot < counts_ref[0]

        @pl.when(listed & (offset == 1))
        def _():
            put(1, slot)

        @pl.when(listed & (offset == -1))
        def _():
            put(2, slot)

        @pl.when(jnp.logical_not(listed))
        def _():
            for k in range(0, bins, zero_ref.shape[0]):
                to = out_hbm.at[0, slot, pl.ds(k, zero_ref.shape[0])]
                pltpu.make_async_copy(zero_ref, to, out_sem).start()

    for slot in range(1, slots):
        @pl.when((slot < counts_ref[0]) & (offsets[slot] == 2))
        def _():
            for k in range(bins):
                both = jnp.dot(left_ref[k], last_ref[k], preferred_element_type=jnp.float32)
                product_ref[k] = both.astype(jnp.bfloat16).reshape(2, channels, channels)
                if k % 2 == 1:
                    part = pl.ds(k - 1, 2)
                    pltpu.make_async_copy(product_ref.at[part], out_hbm.at[0, slot, part], out_sem).start()

    for slot in range(slots):
        pltpu.make_async_copy(made_ref.at[0], out_hbm.at[0, slot], out_sem).wait()


def body(traces, band_bins, partners, partner_counts):
    windows, samples, channels = traces.shape
    bin_count = band_bins.shape[0]
    tm_count = lax.axis_size("tm")
    group = min(128, bin_count)
    groups = bin_count // group
    bins = bin_count // tm_count
    rows = 32 * windows
    chips = tm_count // 2
    depth = 2 * windows * tm_count
    dma = pltpu.SemaphoreType.DMA
    buffer = pltpu.VMEM((tm_count, rows, channels), jnp.bfloat16)
    made, left, last, listed = pl.pallas_call(
        functools.partial(exchange_kernel, tm_count),
        out_shape=[
            pltpu.VMEM((3, bins, 2, channels, channels), jnp.bfloat16),
            pltpu.VMEM((bins, 2 * channels, depth), jnp.bfloat16),
            pltpu.VMEM((bins, depth, channels), jnp.bfloat16),
            pltpu.VMEM(partners.shape, jnp.int32),
        ],
        in_specs=[pl.BlockSpec(memory_space=pltpu.HBM)] * 3,
        out_specs=[pl.BlockSpec(memory_space=pltpu.VMEM)] * 4,
        scratch_shapes=[
            pltpu.VMEM((groups, group), jnp.int32),
            pltpu.VMEM((windows, samples, channels), jnp.bfloat16),
            pltpu.VMEM((2, 2 * group, samples // 2), jnp.bfloat16),
            pltpu.VMEM((groups, 2 * group, windows * channels), jnp.float32),
            buffer, buffer, buffer, buffer, buffer,
            pltpu.VMEM((tm_count * 32, channels), jnp.float32),
            pltpu.VMEM((bins, depth, channels), jnp.bfloat16),
            pltpu.VMEM((tm_count, rows // windows, channels), jnp.bfloat16),
            pltpu.VMEM((tm_count, rows // windows, channels), jnp.bfloat16),
            dma((3,)), dma, dma((chips,)),
            dma, dma((chips,)), dma, dma, dma, dma,
            dma((2,)), dma((2,)), dma((2,)), dma((2,)),
        ],
        compiler_params=pltpu.CompilerParams(
            collective_id=0, has_side_effects=True, vmem_limit_bytes=40 << 20),
        name="exchange",
    )(
        pltpu.with_memory_space_constraint(band_bins.reshape(groups, group), pltpu.HBM),
        pltpu.with_memory_space_constraint(traces, pltpu.HBM),
        pltpu.with_memory_space_constraint(partners, pltpu.HBM),
    )

    return pl.pallas_call(
        place_kernel,
        out_shape=jax.ShapeDtypeStruct((1, 4, bins, 2, channels, channels), jnp.bfloat16),
        in_specs=[pl.BlockSpec(memory_space=pltpu.SMEM)] + [pl.BlockSpec(memory_space=pltpu.VMEM)] * 4,
        out_specs=pl.BlockSpec(memory_space=pl.ANY),
        scratch_shapes=[
            pltpu.VMEM((bins, 2, channels, channels), jnp.bfloat16),
            pltpu.VMEM((bins // 4, 2, channels, channels), jnp.bfloat16),
            pltpu.SemaphoreType.DMA,
        ],
        compiler_params=pltpu.CompilerParams(vmem_limit_bytes=40 << 20),
        name="place",
    )(
        partner_counts, listed, made, left, last,
    )


def solution(mesh):
    placed = (P("tm", None, "chan"), P(), P("chan", None), P("chan"))
    return jax.shard_map(
        body,
        mesh=mesh,
        in_specs=placed,
        out_specs=P("chan", None, "tm", None, None, None),
        check_vma=False,
    )
```
